32 devices in a mesh: req: 16 (over z, x, core), tp: 2 (over y).
Axes of the slice: x: 2, y: 2, z: 4, core: 2. Of those that a mesh axis runs over, the one named last changes fastest.
Arguments:
- queries: bfloat16 [6144, 8192], P('req', 'tp'), may hold values from -40 to 40
- suffix_kv: bfloat16 [2, 6144, 1024], P(None, 'req', 'tp'), may hold values from -4 to 4
- prefix_kv: bfloat16 [2, 16, 256, 1024], P(None, 'req', 'tp'), may hold values from -4 to 4
- suffix_length: int32 [15], replicated, may hold values from 16 to 384, as said below
- request_group: int32 [15], replicated, may hold values from 0 to 3
- request_order: int32 [15], replicated, may hold values from 0 to 14, each once
- owner_map: int32 [16], replicated, may hold values from 0 to 15, each once
Outputs:
- attention: bfloat16 [6144, 8192], P('req', 'tp')
The draws below stay inside these ranges and needn't reach their ends.
Inputs may be any that keep to these rules, and one draw needn't show every extreme that they name: `suffix_length`: every suffix has 16 to 384 tokens; in every draw one suffix has exactly 384 tokens and one exactly 16.
All inputs are finite; a program needn't handle non-finite values.
Results may differ from the reference program's by a relative error of at most 0.007.
Values may be sent and summed in bfloat16 or wider, within the bound.
A program may use at most 128 MiB of HBM per device.

```python
import math
import jax
import jax.numpy as jnp
from jax import lax

QH = 64
KVH = 8
HD = 128
GROUPS = 4
MINLEN = 16
MAXLEN = 384
TOK_DEV = 384
PBLK = 256
REQS = 15
SLOTS = 6144
N_REQ = 16


def shared_rows(key):
    kv_key = jax.random.fold_in(key, 101)
    query_key = jax.random.fold_in(key, 202)
    kv_rows = jnp.clip(jax.random.normal(kv_key, (2, SLOTS, KVH * HD), jnp.float32), -4.0, 4.0)
    query_rows = jnp.clip(jax.random.normal(query_key, (SLOTS, QH * HD), jnp.float32), -4.0, 4.0)
    return (kv_rows, query_rows)


def draw_queries(key, part):
    return shared_rows(key)[1].astype(jnp.bfloat16)


def draw_suffix_kv(key, part):
    return shared_rows(key)[0].astype(jnp.bfloat16)


def draw_suffix_length(key, part):
    lengths = jax.random.randint(jax.random.fold_in(key, 7), (REQS,), MINLEN, MAXLEN + 1)
    longest = jax.random.randint(jax.random.fold_in(key, 8), (), 0, REQS)
    lengths = lengths.at[longest].set(MAXLEN)
    lengths = lengths.at[(longest + 1) % REQS].set(MINLEN)
    return lengths.astype(jnp.int32)


def place_ends(drawn, rng, smallest, top_value):
    dims = drawn.shape
    spot = [jax.random.randint(jax.random.fold_in(rng, axis), (), 0, dims[axis]) for axis in range(len(dims))]
    drawn = drawn.at[tuple(spot)].set(smallest)
    longest = dims.index(max(dims))
    spot[longest] = (spot[longest] + 1) % dims[longest]
    return drawn.at[tuple(spot)].set(top_value)


def block_levels(own_key, extent, split, smallest, high):
    level = 1.0
    for dim, parts in split:
        steps = jax.random.uniform(jax.random.fold_in(jax.random.fold_in(own_key, 6), dim), (parts,), jnp.float32, smallest / len(split), high / len(split))
        level = level * jnp.repeat(jnp.exp(steps), extent[dim] // parts).reshape((-1,) + (1,) * (len(extent) - 1 - dim))
    return level


def scatter_about(own_key, extent, scale, most, shards=(), kind=jnp.bfloat16):
    gain = block_levels(own_key, extent, shards, -0.22, 0.18) if shards else 1.0
    entries = jax.random.normal(own_key, extent, jnp.float32) * scale * gain
    return jnp.minimum(jnp.maximum(entries, -most), most).astype(kind)


def setup_inputs(seed: int = 0) -> dict:
    key_of = jax.random.split(jax.random.key(seed), 8)
    queries = draw_queries(jax.random.fold_in(key_of[7], 71), 0)
    suffix_kv = draw_suffix_kv(jax.random.fold_in(key_of[7], 71), 0)
    prefix_kv = scatter_about(key_of[2], (2, N_REQ, PBLK, KVH * HD), 1.0, 4.0, ((1, 16), (2, 2)))
    suffix_length = draw_suffix_length(jax.random.fold_in(key_of[7], 71), 0)
    request_group = place_ends(jax.random.randint(key_of[4], (REQS,), 0, GROUPS), jax.random.fold_in(key_of[4], 1), 0, GROUPS - 1).astype(jnp.int32)
    request_order = jax.random.permutation(key_of[5], REQS).astype(jnp.int32)
    owner_map = jax.random.permutation(key_of[6], N_REQ).astype(jnp.int32)
    return {"queries": queries, "suffix_kv": suffix_kv, "prefix_kv": prefix_kv, "suffix_length": suffix_length, "request_group": request_group, "request_order": request_order, "owner_map": owner_map}


masked_score = -1e+30

def pack_index(slot_ids, starts, stops):
    inside = (starts[None, :] <= slot_ids[:, None]) & (slot_ids[:, None] < stops[None, :])
    request_ids = jnp.arange(starts.shape[0], dtype=jnp.int32)
    found = lax.optimization_barrier(jnp.sum(jnp.where(inside, request_ids[None, :], 0), axis=1)).astype(jnp.int32)
    missing = jnp.where(jnp.any(inside, axis=1), 0, starts.shape[0]).astype(jnp.int32)
    return (found + missing).astype(jnp.int32)

def reference(queries, suffix_kv, prefix_kv, suffix_length, request_group, request_order, owner_map):
    per_kv = QH // KVH
    score_scale = 1.0 / math.sqrt(HD)
    packed_length = jnp.take(suffix_length, request_order).astype(jnp.int32)
    packed_group = jnp.take(request_group, request_order).astype(jnp.int32)
    starts = ((jnp.arange(REQS, dtype=jnp.int32) + 1) * TOK_DEV - packed_length // 2).astype(jnp.int32)
    stops = (starts + packed_length).astype(jnp.int32)
    block_ids = jnp.arange(N_REQ, dtype=jnp.int32)
    stored_group = lax.optimization_barrier(jnp.sum(jnp.where(owner_map[None, :] == block_ids[:, None], (block_ids // (N_REQ // GROUPS))[None, :], 0), axis=1)).astype(jnp.int32)
    key_group = jnp.repeat(stored_group, PBLK)
    prefix_keys = prefix_kv[0].reshape(N_REQ * PBLK, KVH, HD).astype(jnp.float32)
    prefix_values = prefix_kv[1].reshape(N_REQ * PBLK, KVH, HD).astype(jnp.float32)
    padded = jnp.concatenate([jnp.zeros((2, TOK_DEV, KVH * HD), suffix_kv.dtype), suffix_kv], axis=1)

    def one_device(device):
        first_slot = (device * TOK_DEV).astype(jnp.int32)
        slot_ids = first_slot + jnp.arange(TOK_DEV, dtype=jnp.int32)
        own_pack = pack_index(slot_ids, starts, stops)
        is_live = own_pack < REQS
        slot_group = jnp.take(packed_group, jnp.minimum(own_pack, REQS - 1))
        near_slots = first_slot - TOK_DEV + jnp.arange(2 * TOK_DEV, dtype=jnp.int32)
        near_pack = pack_index(near_slots, starts, stops)
        nearby = lax.dynamic_slice_in_dim(padded, first_slot, 2 * TOK_DEV, 1)
        suffix_visible = (near_pack[None, :] == own_pack[:, None]) & (near_slots[None, :] <= slot_ids[:, None]) & (near_slots[None, :] >= 0)
        prefix_visible = key_group[None, :] == slot_group[:, None]
        visible = jnp.concatenate([prefix_visible, suffix_visible], axis=1) & is_live[:, None]
        query_rows = lax.dynamic_slice_in_dim(queries, first_slot, TOK_DEV, 0).reshape(TOK_DEV, KVH, per_kv, HD).astype(jnp.float32)
        near_keys = nearby[0].reshape(2 * TOK_DEV, KVH, HD).astype(jnp.float32)
        near_values = nearby[1].reshape(2 * TOK_DEV, KVH, HD).astype(jnp.float32)

        def one_head(kv_head):
            head_queries = jnp.take(query_rows, kv_head, axis=1)
            key_rows = jnp.concatenate([jnp.take(prefix_keys, kv_head, axis=1), jnp.take(near_keys, kv_head, axis=1)], axis=0)
            value_rows = jnp.concatenate([jnp.take(prefix_values, kv_head, axis=1), jnp.take(near_values, kv_head, axis=1)], axis=0)
            scores = jnp.einsum('tqd,kd->tqk', head_queries, key_rows) * score_scale
            allowed = visible[:, None, :]
            scores = jnp.where(allowed, scores, masked_score)
            row_max = lax.optimization_barrier(jnp.max(scores, axis=-1, keepdims=True))
            weights = jnp.where(allowed, jnp.exp(scores - row_max), 0.0)
            row_sum = lax.optimization_barrier(jnp.sum(weights, axis=-1))
            rounded = lax.optimization_barrier(weights.astype(jnp.bfloat16)).astype(jnp.float32)
            weighted = jnp.einsum('tqk,kd->tqd', rounded, value_rows)
            divisor = jnp.where(is_live[:, None], row_sum, 1.0)
            return jnp.where(is_live[:, None, None], weighted / divisor[..., None], 0.0)
        heads_out = lax.map(one_head, jnp.arange(KVH, dtype=jnp.int32))
        return jnp.transpose(heads_out, (1, 0, 2, 3)).reshape(TOK_DEV, QH * HD).astype(jnp.bfloat16)
    outputs = lax.map(one_device, jnp.arange(N_REQ, dtype=jnp.int32))
    return outputs.reshape(SLOTS, QH * HD)
```

```python
import functools
import math

import jax
import jax.numpy as jnp
from jax import lax
from jax.experimental import pallas as pl
from jax.experimental.pallas import tpu as pltpu
from jax.sharding import PartitionSpec as P

QH = 64
KVH = 8
HD = 128
GROUPS = 4
PER_KV = QH // KVH
PAIR = 2
UP, DOWN, ACROSS, SIBLING = range(4)

masked_score = -1e30
to_exp2 = math.log2(math.e) / math.sqrt(HD)


def nt_dot(a, b):
    return lax.dot_general(a, b, (((1,), (1,)), ((), ())), preferred_element_type=jnp.float32)


def kernel(
    reqs, tps, heads,
    queries, suffix, prefix, lengths, groups, order, owners,
    out,
    *scratch,
):
    stored = scratch[:heads]
    (before, key_stage, value_stage, bias,
     unit_send, unit_recv, peer_send, peer_recv, own_sem, before_send, before_recv) = scratch[heads:]
    me = lax.axis_index("req")
    tp = lax.axis_index("tp")
    layers = reqs // 4
    z, x, core = me // 4, (me // 2) % 2, me % 2
    half_rows = queries.shape[0] // 2
    block_rows = stored[0].shape[2]
    part_rows = block_rows // tps
    per_group = reqs // GROUPS
    prefix_rows = per_group * block_rows
    across = z * 4 + (1 - x) * 2 + core
    sibling = z * 4 + x * 2 + 1 - core
    targets = {UP: me + 4, DOWN: me - 4, ACROSS: across, SIBLING: sibling}

    barrier = pltpu.get_barrier_semaphore()

    def greet(there, **device):
        @pl.when(there)
        def _():
            pl.semaphore_signal(barrier, inc=1, device_id=device, device_id_type=pl.DeviceIdType.MESH)

        return jnp.where(there, 1, 0)

    met = (
        greet(z + 1 < layers, req=me + 4)
        + greet(z > 0, req=me - 4)
        + greet(z >= 0, req=across)
        + greet(z >= 0, req=sibling)
        + greet((core == 1) & (me + 1 < reqs), req=me + 1)
        + greet((core == 0) & (me > 0), req=me - 1)
    )
    for k in range(1, tps):
        met = met + greet(z >= 0, tp=(tp + k) % tps)
    pl.semaphore_wait(barrier, met)

    def unit_copy(h, block, way):
        return pltpu.make_async_remote_copy(
            src_ref=stored[h].at[block],
            dst_ref=stored[h].at[block],
            send_sem=unit_send.at[h, block, way],
            recv_sem=unit_recv.at[h, block],
            device_id={"req": targets[way]},
            device_id_type=pl.DeviceIdType.MESH,
        )

    def peer_copy(h, peer, part):
        columns = pl.ds(pl.multiple_of((peer * heads + h) * HD, HD), HD)
        return pltpu.make_async_remote_copy(
            src_ref=prefix.at[:, 0, :, columns],
            dst_ref=stored[h].at[me, :, pl.ds(pl.multiple_of(part * part_rows, part_rows), part_rows), :],
            send_sem=peer_send.at[h, peer],
            recv_sem=peer_recv.at[h, part],
            device_id={"tp": peer},
            device_id_type=pl.DeviceIdType.MESH,
        )

    def own_copy(h):
        columns = pl.ds(pl.multiple_of((tp * heads + h) * HD, HD), HD)
        return pltpu.make_async_copy(
            prefix.at[:, 0, :, columns],
            stored[h].at[me, :, pl.ds(pl.multiple_of(tp * part_rows, part_rows), part_rows), :],
            own_sem.at[h],
        )

    before_copy = pltpu.make_async_remote_copy(
        src_ref=suffix.at[:, pl.ds(half_rows, half_rows), :],
        dst_ref=before,
        send_sem=before_send,
        recv_sem=before_recv,
        device_id={"req": me + 1},
        device_id_type=pl.DeviceIdType.MESH,
    )

    def pass_on(h, block, ways):
        for way, there in ways:
            @pl.when(there)
            def _(way=way):
                unit_copy(h, block, way).start()

    def send_own(h):
        own_copy(h).wait()
        for k in range(1, tps):
            peer_copy(h, (tp + k) % tps, (tp + k) % tps).wait_recv()
        pass_on(h, me, [(UP, z + 1 < layers), (DOWN, z > 0), (ACROSS, z >= 0), (SIBLING, z >= 0)])

    def from_layer(h, step):
        below, above = z - step, z + step

        @pl.when(below >= 0)
        def _():
            block = me - 4 * step
            unit_copy(h, block, UP).wait_recv()
            pass_on(h, block, [(UP, z + 1 < layers), (ACROSS, z >= 0), (SIBLING, z >= 0)])

        @pl.when(above < layers)
        def _():
            block = me + 4 * step
            unit_copy(h, block, DOWN).wait_recv()
            pass_on(h, block, [(DOWN, z > 0), (ACROSS, z >= 0), (SIBLING, z >= 0)])

    def from_across(h, step):
        below, above = z - step, z + step

        @pl.when(below >= 0)
        def _():
            unit_copy(h, across - 4 * step, ACROSS).wait_recv()
            unit_copy(h, across - 4 * step, SIBLING).start()

        @pl.when((above < layers) & (step > 0))
        def _():
            unit_copy(h, across + 4 * step, ACROSS).wait_recv()
            unit_copy(h, across + 4 * step, SIBLING).start()

    def relay(h, step):
        @pl.when(step < layers)
        def _():
            from_layer(h, step)

        from_across(h, step - 1)

    def from_sibling(h):
        @pl.loop(0, reqs // 2)
        def _(i):
            unit_copy(h, i * 2 + 1 - core, SIBLING).wait_recv()

    for h in range(heads):
        own_copy(h).start()
        for k in range(1, tps):
            peer_copy(h, (tp + k) % tps, tp).start()
    send_own(0)

    @pl.when(me + 1 < reqs)
    def _():
        before_copy.start()

    if heads > 1:
        send_own(1)

    tail = order[jnp.maximum(me - 1, 0)]
    head = order[jnp.minimum(me, reqs - 2)]
    tail_length = jnp.where(me > 0, lengths[tail], 0)
    head_length = jnp.where(me + 1 < reqs, lengths[head], 0)
    group_of = (groups[tail], groups[head])
    tail_live = tail_length - tail_length // 2
    tail_first = half_rows - tail_length // 2
    head_first = half_rows - head_length // 2
    near = bias.shape[2]
    head_near = 4 * half_rows // 3
    row = lax.broadcasted_iota(jnp.int32, (half_rows, near), 0)
    column = lax.broadcasted_iota(jnp.int32, (half_rows, near), 1)
    seen = (column >= tail_first) & (column - half_rows <= row)
    bias[0] = jnp.where(seen, 0.0, masked_score)
    own_column = column - (head_near - half_rows)
    seen = (own_column >= head_first) & (own_column <= row)
    bias[1] = jnp.where(seen, 0.0, masked_score)
    slot = lax.broadcasted_iota(jnp.int32, (half_rows, HD), 0)
    value_stage[:, HD:] = jnp.ones((value_stage.shape[0], HD), value_stage.dtype)

    @pl.when(me == 0)
    def _():
        before[...] = jnp.zeros(before.shape, before.dtype)

    for step in range(1, layers + 1):
        relay(0, step)

    @pl.when(me > 0)
    def _():
        before_copy.wait_recv()

    chunks = PER_KV // PAIR
    slots = 2 * chunks
    for h in range(heads):
        from_sibling(h)
        own_columns = slice(h * HD, (h + 1) * HD)
        if h + 2 < heads:
            send_own(h + 2)
        for half in range(2):
            for i in range(per_group):
                block = owners[group_of[half] * per_group + i]
                rows = slice(i * block_rows, (i + 1) * block_rows)
                key_stage[rows, :] = stored[h][block, 0]
                value_stage[rows, :HD] = stored[h][block, 1]
            if half == 0:
                near_rows = near
                for kind, stage in ((0, key_stage), (1, value_stage)):
                    stage[prefix_rows:prefix_rows + half_rows, :HD] = before[kind, :, own_columns]
                    stage[prefix_rows + half_rows:, :HD] = suffix[kind, :half_rows, own_columns]
            else:
                near_rows = head_near
                for kind, stage in ((0, key_stage), (1, value_stage)):
                    stage[prefix_rows:prefix_rows + near_rows, :HD] = suffix[
                        kind, 2 * half_rows - near_rows:, own_columns
                    ]
            live = slot < tail_live if half == 0 else slot >= head_first

            @pl.loop(0, chunks)
            def _(i, half=half, near_rows=near_rows, live=live, h=h):
                span = pl.ds(half * half_rows, half_rows)
                first = (h * PER_KV + i * PAIR) * HD
                places = [pl.ds(pl.multiple_of(first + k * HD, HD), HD) for k in range(PAIR)]
                query = jnp.concatenate([queries[span, place] for place in places], axis=0)
                far = nt_dot(query, key_stage[:prefix_rows, :])
                close = nt_dot(query, key_stage[prefix_rows:prefix_rows + near_rows, :])
                shade = bias[half][:, :near_rows]
                close = close + jnp.concatenate([shade] * PAIR, axis=0)
                top = jnp.maximum(
                    jnp.max(far, axis=1, keepdims=True), jnp.max(close, axis=1, keepdims=True)
                ) * to_exp2
                far = jnp.exp2(far * to_exp2 - top).astype(jnp.bfloat16)
                close = jnp.exp2(close * to_exp2 - top).astype(jnp.bfloat16)
                total = jnp.dot(far, value_stage[:prefix_rows, :], preferred_element_type=jnp.float32)
                total = total + jnp.dot(
                    close, value_stage[prefix_rows:prefix_rows + near_rows, :],
                    preferred_element_type=jnp.float32,
                )
                for k, place in enumerate(places):
                    part = total[k * half_rows:(k + 1) * half_rows]
                    result = jnp.where(live, part[:, :HD] / part[:, HD:], 0.0)
                    out[span, place] = result.astype(out.dtype)
                if h + 1 < heads:
                    done = (half * chunks + i + 1) * layers
                    for k in range(1, max(1, layers // slots) + 1):
                        @pl.when(done % slots == 0)
                        def _(k=k):
                            relay(h + 1, done // slots - max(1, layers // slots) + k)

    @pl.when(me + 1 < reqs)
    def _():
        before_copy.wait_send()

    for h in range(heads):
        for k in range(1, tps):
            peer_copy(h, (tp + k) % tps, tp).wait_send()

        @pl.loop(0, layers)
        def _(layer, h=h):
            mine = layer * 4 + x * 2 + core

            @pl.when((layer <= z) & (z + 1 < layers))
            def _():
                unit_copy(h, mine, UP).wait_send()

            @pl.when((layer >= z) & (z > 0))
            def _():
                unit_copy(h, mine, DOWN).wait_send()

            unit_copy(h, mine, ACROSS).wait_send()
            unit_copy(h, mine, SIBLING).wait_send()
            unit_copy(h, layer * 4 + (1 - x) * 2 + core, SIBLING).wait_send()


def per_device(reqs, tps, queries, suffix, prefix, lengths, groups, order, owners):
    heads = suffix.shape[2] // HD
    rows = queries.shape[0]
    half = rows // 2
    block_rows = prefix.shape[2] * tps
    keys = reqs // GROUPS * block_rows + rows
    vmem = pl.BlockSpec(memory_space=pltpu.VMEM)
    smem = pl.BlockSpec(memory_space=pltpu.SMEM)
    return pl.pallas_call(
        functools.partial(kernel, reqs, tps, heads),
        out_shape=jax.ShapeDtypeStruct(queries.shape, queries.dtype),
        in_specs=[vmem] * 3 + [smem] * 4,
        out_specs=vmem,
        scratch_shapes=[pltpu.VMEM((reqs, 2, block_rows, HD), jnp.bfloat16)] * heads + [
            pltpu.VMEM((2, half, suffix.shape[2]), jnp.bfloat16),
            pltpu.VMEM((keys, HD), jnp.bfloat16),
            pltpu.VMEM((keys, 2 * HD), jnp.bfloat16),
            pltpu.VMEM((2, half, rows), jnp.float32),
            pltpu.SemaphoreType.DMA((heads, reqs, 4)),
            pltpu.SemaphoreType.DMA((heads, reqs)),
            pltpu.SemaphoreType.DMA((heads, tps)),
            pltpu.SemaphoreType.DMA((heads, tps)),
            pltpu.SemaphoreType.DMA((heads,)),
            pltpu.SemaphoreType.DMA,
            pltpu.SemaphoreType.DMA,
        ],
        compiler_params=pltpu.CompilerParams(
            collective_id=0, has_side_effects=True, vmem_limit_bytes=56 * 1024 * 1024
        ),
        cost_estimate=pl.CostEstimate(
            flops=4 * rows * heads * PER_KV * HD * keys,
            bytes_accessed=4 * queries.size,
            transcendentals=rows * heads * PER_KV * keys,
        ),
    )(queries, suffix, prefix, lengths, groups, order, owners)


def solution(mesh):
    in_specs = (
        P("req", "tp"),
        P(None, "req", "tp"),
        P(None, "req", "tp", None),
        P(),
        P(),
        P(),
        P(),
    )
    body = functools.partial(per_device, mesh.shape["req"], mesh.shape["tp"])
    return jax.shard_map(
        body, mesh=mesh, in_specs=in_specs, out_specs=P("req", "tp"), check_vma=False
    )
```

```python
import functools
import math

import jax
import jax.numpy as jnp
from jax import lax
from jax.experimental import pallas as pl
from jax.experimental.pallas import tpu as pltpu
from jax.sharding import PartitionSpec as P

QH = 64
KVH = 8
HD = 128
GROUPS = 4
PER_KV = QH // KVH
PAIR = 2
STREAMS = 2
UP, DOWN, ACROSS, SIBLING = range(4)

masked_score = -1e30
to_exp2 = math.log2(math.e) / math.sqrt(HD)


def nt_dot(a, b):
    return lax.dot_general(a, b, (((1,), (1,)), ((), ())), preferred_element_type=jnp.float32)


def kernel(
    reqs, tps, heads,
    queries, suffix, prefix, lengths, groups, order, owners,
    out,
    *scratch,
):
    stored = scratch[:heads]
    (before, key_stage, value_stage, bias,
     unit_send, unit_recv, peer_send, peer_recv, own_sem, before_send, before_recv) = scratch[heads:]
    me = lax.axis_index("req")
    tp = lax.axis_index("tp")
    layers = reqs // 4
    z, x, core = me // 4, (me // 2) % 2, me % 2
    half_rows = queries.shape[0] // 2
    block_rows = stored[0].shape[2]
    part_rows = block_rows // tps
    per_group = reqs // GROUPS
    prefix_rows = per_group * block_rows
    across = z * 4 + (1 - x) * 2 + core
    sibling = z * 4 + x * 2 + 1 - core
    targets = {UP: me + 4, DOWN: me - 4, ACROSS: across, SIBLING: sibling}

    barrier = pltpu.get_barrier_semaphore()

    def greet(there, **device):
        @pl.when(there)
        def _():
            pl.semaphore_signal(barrier, inc=1, device_id=device, device_id_type=pl.DeviceIdType.MESH)

        return jnp.where(there, 1, 0)

    met = (
        greet(z + 1 < layers, req=me + 4)
        + greet(z > 0, req=me - 4)
        + greet(z >= 0, req=across)
        + greet(z >= 0, req=sibling)
        + greet((core == 1) & (me + 1 < reqs), req=me + 1)
        + greet((core == 0) & (me > 0), req=me - 1)
    )
    for k in range(1, tps):
        met = met + greet(z >= 0, tp=(tp + k) % tps)
    pl.semaphore_wait(barrier, met)

    def unit_copy(h, block, way):
        return pltpu.make_async_remote_copy(
            src_ref=stored[h].at[block],
            dst_ref=stored[h].at[block],
            send_sem=unit_send.at[h, block, way],
            recv_sem=unit_recv.at[h, block],
            device_id={"req": targets[way]},
            device_id_type=pl.DeviceIdType.MESH,
        )

    def peer_copy(h, peer, part):
        columns = pl.ds(pl.multiple_of((peer * heads + h) * HD, HD), HD)
        return pltpu.make_async_remote_copy(
            src_ref=prefix.at[:, 0, :, columns],
            dst_ref=stored[h].at[me, :, pl.ds(pl.multiple_of(part * part_rows, part_rows), part_rows), :],
            send_sem=peer_send.at[h, peer],
            recv_sem=peer_recv.at[h, part],
            device_id={"tp": peer},
            device_id_type=pl.DeviceIdType.MESH,
        )

    def own_copy(h):
        columns = pl.ds(pl.multiple_of((tp * heads + h) * HD, HD), HD)
        return pltpu.make_async_copy(
            prefix.at[:, 0, :, columns],
            stored[h].at[me, :, pl.ds(pl.multiple_of(tp * part_rows, part_rows), part_rows), :],
            own_sem.at[h],
        )

    before_copy = pltpu.make_async_remote_copy(
        src_ref=suffix.at[:, pl.ds(half_rows, half_rows), :],
        dst_ref=before,
        send_sem=before_send,
        recv_sem=before_recv,
        device_id={"req": me + 1},
        device_id_type=pl.DeviceIdType.MESH,
    )

    def pass_on(h, block, ways):
        for way, there in ways:
            @pl.when(there)
            def _(way=way):
                unit_copy(h, block, way).start()

    def send_own(h):
        own_copy(h).wait()
        for k in range(1, tps):
            peer_copy(h, (tp + k) % tps, (tp + k) % tps).wait_recv()
        pass_on(h, me, [(UP, z + 1 < layers), (DOWN, z > 0), (ACROSS, z >= 0), (SIBLING, z >= 0)])

    def from_layer(h, step):
        below, above = z - step, z + step

        @pl.when(below >= 0)
        def _():
            block = me - 4 * step
            unit_copy(h, block, UP).wait_recv()
            pass_on(h, block, [(UP, z + 1 < layers), (ACROSS, z >= 0), (SIBLING, z >= 0)])

        @pl.when(above < layers)
        def _():
            block = me + 4 * step
            unit_copy(h, block, DOWN).wait_recv()
            pass_on(h, block, [(DOWN, z > 0), (ACROSS, z >= 0), (SIBLING, z >= 0)])

    def from_across(h, step):
        below, above = z - step, z + step

        @pl.when(below >= 0)
        def _():
            unit_copy(h, across - 4 * step, ACROSS).wait_recv()
            unit_copy(h, across - 4 * step, SIBLING).start()

        @pl.when((above < layers) & (step > 0))
        def _():
            unit_copy(h, across + 4 * step, ACROSS).wait_recv()
            unit_copy(h, across + 4 * step, SIBLING).start()

    def relay(h, step):
        @pl.when(step < layers)
        def _():
            from_layer(h, step)

        from_across(h, step - 1)

    def from_sibling(h):
        @pl.loop(0, reqs // 2)
        def _(i):
            unit_copy(h, i * 2 + 1 - core, SIBLING).wait_recv()

    for h in range(heads):
        own_copy(h).start()
        for k in range(1, tps):
            peer_copy(h, (tp + k) % tps, tp).start()
    send_own(0)

    @pl.when(me + 1 < reqs)
    def _():
        before_copy.start()

    if heads > 1:
        send_own(1)

    tail = order[jnp.maximum(me - 1, 0)]
    head = order[jnp.minimum(me, reqs - 2)]
    tail_length = jnp.where(me > 0, lengths[tail], 0)
    head_length = jnp.where(me + 1 < reqs, lengths[head], 0)
    group_of = (groups[tail], groups[head])
    tail_live = tail_length - tail_length // 2
    tail_first = half_rows - tail_length // 2
    head_first = half_rows - head_length // 2
    near = bias.shape[2]
    head_near = 4 * half_rows // 3
    row = lax.broadcasted_iota(jnp.int32, (half_rows, near), 0)
    column = lax.broadcasted_iota(jnp.int32, (half_rows, near), 1)
    seen = (column >= tail_first) & (column - half_rows <= row)
    bias[0] = jnp.where(seen, 0.0, masked_score)
    own_column = column - (head_near - half_rows)
    seen = (own_column >= head_first) & (own_column <= row)
    bias[1] = jnp.where(seen, 0.0, masked_score)
    slot = lax.broadcasted_iota(jnp.int32, (half_rows, HD), 0)
    value_stage[:, HD:] = jnp.ones((value_stage.shape[0], HD), value_stage.dtype)

    @pl.when(me == 0)
    def _():
        before[...] = jnp.zeros(before.shape, before.dtype)

    for step in range(1, layers + 1):
        relay(0, step)

    @pl.when(me > 0)
    def _():
        before_copy.wait_recv()

    chunks = PER_KV // (PAIR * STREAMS)
    slots = 2 * chunks
    for h in range(heads):
        from_sibling(h)
        own_columns = slice(h * HD, (h + 1) * HD)
        if h + 2 < heads:
            send_own(h + 2)
        for half in range(2):
            for i in range(per_group):
                block = owners[group_of[half] * per_group + i]
                rows = slice(i * block_rows, (i + 1) * block_rows)
                key_stage[rows, :] = stored[h][block, 0]
                value_stage[rows, :HD] = stored[h][block, 1]
            if half == 0:
                near_rows = near
                for kind, stage in ((0, key_stage), (1, value_stage)):
                    stage[prefix_rows:prefix_rows + half_rows, :HD] = before[kind, :, own_columns]
                    stage[prefix_rows + half_rows:, :HD] = suffix[kind, :half_rows, own_columns]
            else:
                near_rows = head_near
                for kind, stage in ((0, key_stage), (1, value_stage)):
                    stage[prefix_rows:prefix_rows + near_rows, :HD] = suffix[
                        kind, 2 * half_rows - near_rows:, own_columns
                    ]
            live = slot < tail_live if half == 0 else slot >= head_first

            @pl.loop(0, chunks)
            def _(i, half=half, near_rows=near_rows, live=live, h=h):
                span = pl.ds(half * half_rows, half_rows)
                first = (h * PER_KV + i * PAIR * STREAMS) * HD
                places = [
                    pl.ds(pl.multiple_of(first + k * HD, HD), HD) for k in range(PAIR * STREAMS)
                ]
                shade = jnp.concatenate([bias[half][:, :near_rows]] * PAIR, axis=0)
                scores = []
                for stream in range(STREAMS):
                    pair = places[stream * PAIR:(stream + 1) * PAIR]
                    query = jnp.concatenate([queries[span, place] for place in pair], axis=0)
                    far = nt_dot(query, key_stage[:prefix_rows, :])
                    close = nt_dot(query, key_stage[prefix_rows:prefix_rows + near_rows, :])
                    scores.append((far, close + shade))
                for stream in range(STREAMS):
                    pair = places[stream * PAIR:(stream + 1) * PAIR]
                    far, close = scores[stream]
                    top = jnp.maximum(
                        jnp.max(far, axis=1, keepdims=True), jnp.max(close, axis=1, keepdims=True)
                    ) * to_exp2
                    far = jnp.exp2(far * to_exp2 - top).astype(jnp.bfloat16)
                    close = jnp.exp2(close * to_exp2 - top).astype(jnp.bfloat16)
                    total = jnp.dot(
                        far, value_stage[:prefix_rows, :], preferred_element_type=jnp.float32
                    )
                    total = total + jnp.dot(
                        close, value_stage[prefix_rows:prefix_rows + near_rows, :],
                        preferred_element_type=jnp.float32,
                    )
                    for k, place in enumerate(pair):
                        part = total[k * half_rows:(k + 1) * half_rows]
                        result = jnp.where(live, part[:, :HD] / part[:, HD:], 0.0)
                        out[span, place] = result.astype(out.dtype)
                if h + 1 < heads:
                    done = (half * chunks + i + 1) * layers
                    for k in range(1, max(1, layers // slots) + 1):
                        @pl.when(done % slots == 0)
                        def _(k=k):
                            relay(h + 1, done // slots - max(1, layers // slots) + k)

    @pl.when(me + 1 < reqs)
    def _():
        before_copy.wait_send()

    for h in range(heads):
        for k in range(1, tps):
            peer_copy(h, (tp + k) % tps, tp).wait_send()

        @pl.loop(0, layers)
        def _(layer, h=h):
            mine = layer * 4 + x * 2 + core

            @pl.when((layer <= z) & (z + 1 < layers))
            def _():
                unit_copy(h, mine, UP).wait_send()

            @pl.when((layer >= z) & (z > 0))
            def _():
                unit_copy(h, mine, DOWN).wait_send()

            unit_copy(h, mine, ACROSS).wait_send()
            unit_copy(h, mine, SIBLING).wait_send()
            unit_copy(h, layer * 4 + (1 - x) * 2 + core, SIBLING).wait_send()


def per_device(reqs, tps, queries, suffix, prefix, lengths, groups, order, owners):
    heads = suffix.shape[2] // HD
    rows = queries.shape[0]
    half = rows // 2
    block_rows = prefix.shape[2] * tps
    keys = reqs // GROUPS * block_rows + rows
    vmem = pl.BlockSpec(memory_space=pltpu.VMEM)
    smem = pl.BlockSpec(memory_space=pltpu.SMEM)
    return pl.pallas_call(
        functools.partial(kernel, reqs, tps, heads),
        out_shape=jax.ShapeDtypeStruct(queries.shape, queries.dtype),
        in_specs=[vmem] * 3 + [smem] * 4,
        out_specs=vmem,
        scratch_shapes=[pltpu.VMEM((reqs, 2, block_rows, HD), jnp.bfloat16)] * heads + [
            pltpu.VMEM((2, half, suffix.shape[2]), jnp.bfloat16),
            pltpu.VMEM((keys, HD), jnp.bfloat16),
            pltpu.VMEM((keys, 2 * HD), jnp.bfloat16),
            pltpu.VMEM((2, half, rows), jnp.float32),
            pltpu.SemaphoreType.DMA((heads, reqs, 4)),
            pltpu.SemaphoreType.DMA((heads, reqs)),
            pltpu.SemaphoreType.DMA((heads, tps)),
            pltpu.SemaphoreType.DMA((heads, tps)),
            pltpu.SemaphoreType.DMA((heads,)),
            pltpu.SemaphoreType.DMA,
            pltpu.SemaphoreType.DMA,
        ],
        compiler_params=pltpu.CompilerParams(
            collective_id=0, has_side_effects=True, vmem_limit_bytes=56 * 1024 * 1024
        ),
        cost_estimate=pl.CostEstimate(
            flops=4 * rows * heads * PER_KV * HD * keys,
            bytes_accessed=4 * queries.size,
            transcendentals=rows * heads * PER_KV * keys,
        ),
    )(queries, suffix, prefix, lengths, groups, order, owners)


def solution(mesh):
    in_specs = (
        P("req", "tp"),
        P(None, "req", "tp"),
        P(None, "req", "tp", None),
        P(),
        P(),
        P(),
        P(),
    )
    body = functools.partial(per_device, mesh.shape["req"], mesh.shape["tp"])
    return jax.shard_map(
        body, mesh=mesh, in_specs=in_specs, out_specs=P("req", "tp"), check_vma=False
    )
```

```python
import functools
import math

import jax
import jax.numpy as jnp
from jax import lax
from jax.experimental import pallas as pl
from jax.experimental.pallas import tpu as pltpu
from jax.sharding import PartitionSpec as P

QH = 64
KVH = 8
HD = 128
GROUPS = 4
PER_KV = QH // KVH
PAIR = 2
STREAMS = 2
UP, DOWN, ACROSS, SIBLING = range(4)

masked_score = -1e30
to_exp2 = math.log2(math.e) / math.sqrt(HD)


def nt_dot(a, b):
    return lax.dot_general(a, b, (((1,), (1,)), ((), ())), preferred_element_type=jnp.float32)


def kernel(
    reqs, tps, heads,
    queries, suffix, prefix, lengths, groups, order, owners,
    out,
    *scratch,
):
    stored = scratch[:heads]
    (before, key_stage, value_stage, bias,
     unit_send, unit_recv, peer_send, peer_recv, own_sem, before_send, before_recv) = scratch[heads:]
    me = lax.axis_index("req")
    tp = lax.axis_index("tp")
    layers = reqs // 4
    z, x, core = me // 4, (me // 2) % 2, me % 2
    half_rows = queries.shape[0] // 2
    block_rows = stored[0].shape[2]
    part_rows = block_rows // tps
    per_group = reqs // GROUPS
    prefix_rows = per_group * block_rows
    across = z * 4 + (1 - x) * 2 + core
    sibling = z * 4 + x * 2 + 1 - core
    targets = {UP: me + 4, DOWN: me - 4, ACROSS: across, SIBLING: sibling}

    barrier = pltpu.get_barrier_semaphore()

    def greet(there, **device):
        @pl.when(there)
        def _():
            pl.semaphore_signal(barrier, inc=1, device_id=device, device_id_type=pl.DeviceIdType.MESH)

        return jnp.where(there, 1, 0)

    met = (
        greet(z + 1 < layers, req=me + 4)
        + greet(z > 0, req=me - 4)
        + greet(z >= 0, req=across)
        + greet(z >= 0, req=sibling)
        + greet((core == 1) & (me + 1 < reqs), req=me + 1)
        + greet((core == 0) & (me > 0), req=me - 1)
    )
    for k in range(1, tps):
        met = met + greet(z >= 0, tp=(tp + k) % tps)
    pl.semaphore_wait(barrier, met)

    def unit_copy(h, block, way):
        return pltpu.make_async_remote_copy(
            src_ref=stored[h].at[block],
            dst_ref=stored[h].at[block],
            send_sem=unit_send.at[h, block, way],
            recv_sem=unit_recv.at[h, block],
            device_id={"req": targets[way]},
            device_id_type=pl.DeviceIdType.MESH,
        )

    def peer_copy(h, peer, part):
        columns = pl.ds(pl.multiple_of((peer * heads + h) * HD, HD), HD)
        return pltpu.make_async_remote_copy(
            src_ref=prefix.at[:, 0, :, columns],
            dst_ref=stored[h].at[me, :, pl.ds(pl.multiple_of(part * part_rows, part_rows), part_rows), :],
            send_sem=peer_send.at[h, peer],
            recv_sem=peer_recv.at[h, part],
            device_id={"tp": peer},
            device_id_type=pl.DeviceIdType.MESH,
        )

    def own_copy(h):
        columns = pl.ds(pl.multiple_of((tp * heads + h) * HD, HD), HD)
        return pltpu.make_async_copy(
            prefix.at[:, 0, :, columns],
            stored[h].at[me, :, pl.ds(pl.multiple_of(tp * part_rows, part_rows), part_rows), :],
            own_sem.at[h],
        )

    before_copy = pltpu.make_async_remote_copy(
        src_ref=suffix.at[:, pl.ds(half_rows, half_rows), :],
        dst_ref=before,
        send_sem=before_send,
        recv_sem=before_recv,
        device_id={"req": me + 1},
        device_id_type=pl.DeviceIdType.MESH,
    )

    def pass_on(h, block, ways):
        for way, there in ways:
            @pl.when(there)
            def _(way=way):
                unit_copy(h, block, way).start()

    def send_own(h):
        own_copy(h).wait()
        for k in range(1, tps):
            peer_copy(h, (tp + k) % tps, (tp + k) % tps).wait_recv()
        pass_on(h, me, [(UP, z + 1 < layers), (DOWN, z > 0), (ACROSS, z >= 0), (SIBLING, z >= 0)])

    def from_layer(h, step):
        below, above = z - step, z + step

        @pl.when(below >= 0)
        def _():
            block = me - 4 * step
            unit_copy(h, block, UP).wait_recv()
            pass_on(h, block, [(UP, z + 1 < layers), (ACROSS, z >= 0), (SIBLING, z >= 0)])

        @pl.when(above < layers)
        def _():
            block = me + 4 * step
            unit_copy(h, block, DOWN).wait_recv()
            pass_on(h, block, [(DOWN, z > 0), (ACROSS, z >= 0), (SIBLING, z >= 0)])

    def from_across(h, step):
        below, above = z - step, z + step

        @pl.when(below >= 0)
        def _():
            unit_copy(h, across - 4 * step, ACROSS).wait_recv()
            unit_copy(h, across - 4 * step, SIBLING).start()

        @pl.when((above < layers) & (step > 0))
        def _():
            unit_copy(h, across + 4 * step, ACROSS).wait_recv()
            unit_copy(h, across + 4 * step, SIBLING).start()

    def relay(h, step):
        @pl.when(step < layers)
        def _():
            from_layer(h, step)

        from_across(h, step - 1)

    def from_sibling(h):
        @pl.loop(0, reqs // 2)
        def _(i):
            unit_copy(h, i * 2 + 1 - core, SIBLING).wait_recv()

    for h in range(heads):
        own_copy(h).start()
        for k in range(1, tps):
            peer_copy(h, (tp + k) % tps, tp).start()
    send_own(0)

    @pl.when(me + 1 < reqs)
    def _():
        before_copy.start()

    if heads > 1:
        send_own(1)

    tail = order[jnp.maximum(me - 1, 0)]
    head = order[jnp.minimum(me, reqs - 2)]
    tail_length = jnp.where(me > 0, lengths[tail], 0)
    head_length = jnp.where(me + 1 < reqs, lengths[head], 0)
    group_of = (groups[tail], groups[head])
    tail_live = tail_length - tail_length // 2
    tail_first = half_rows - tail_length // 2
    head_first = half_rows - head_length // 2
    near = bias.shape[2]
    head_near = 4 * half_rows // 3
    row = lax.broadcasted_iota(jnp.int32, (half_rows, near), 0)
    column = lax.broadcasted_iota(jnp.int32, (half_rows, near), 1)
    seen = (column >= tail_first) & (column - half_rows <= row)
    bias[0] = jnp.where(seen, 0.0, masked_score)
    own_column = column - (head_near - half_rows)
    seen = (own_column >= head_first) & (own_column <= row)
    bias[1] = jnp.where(seen, 0.0, masked_score)
    slot = lax.broadcasted_iota(jnp.int32, (half_rows, HD), 0)
    value_stage[:, HD:] = jnp.ones((value_stage.shape[0], HD), value_stage.dtype)

    @pl.when(me == 0)
    def _():
        before[...] = jnp.zeros(before.shape, before.dtype)

    for step in range(1, layers + 1):
        relay(0, step)

    @pl.when(me > 0)
    def _():
        before_copy.wait_recv()

    chunks = PER_KV // (PAIR * STREAMS)
    slots = 2 * chunks
    for h in range(heads):
        from_sibling(h)
        own_columns = slice(h * HD, (h + 1) * HD)
        if h + 2 < heads:
            send_own(h + 2)
        for half in range(2):
            for i in range(per_group):
                block = owners[group_of[half] * per_group + i]
                rows = slice(i * block_rows, (i + 1) * block_rows)
                turned = stored[h][block, 0].T
                key_stage[:HD, rows] = turned
                key_stage[HD:, rows] = turned
                value_stage[rows, :HD] = stored[h][block, 1]
            near_rows = near if half == 0 else head_near
            if half == 0:
                close = [
                    jnp.concatenate(
                        [before[kind, :, own_columns], suffix[kind, :half_rows, own_columns]], axis=0
                    ) for kind in range(2)
                ]
            else:
                close = [suffix[kind, 2 * half_rows - near_rows:, own_columns] for kind in range(2)]
            rows = slice(prefix_rows, prefix_rows + near_rows)
            turned = close[0].T
            key_stage[:HD, rows] = turned
            key_stage[HD:, rows] = turned
            value_stage[rows, :HD] = close[1]
            live = slot < tail_live if half == 0 else slot >= head_first

            @pl.loop(0, chunks)
            def _(i, half=half, near_rows=near_rows, live=live, h=h):
                span = pl.ds(half * half_rows, half_rows)
                first = (h * PER_KV + i * PAIR * STREAMS) * HD
                places = [
                    pl.ds(pl.multiple_of(first + k * HD, HD), HD) for k in range(PAIR * STREAMS)
                ]
                shade = jnp.concatenate([bias[half][:, :near_rows]] * PAIR, axis=0)
                rows = prefix_rows + near_rows
                scores = []
                for stream in range(STREAMS):
                    pair = places[stream * PAIR:(stream + 1) * PAIR]
                    query = jnp.concatenate([queries[span, place] for place in pair], axis=0)
                    query = query.astype(jnp.float32) * to_exp2
                    high = query.astype(jnp.bfloat16)
                    low = (query - high.astype(jnp.float32)).astype(jnp.bfloat16)
                    scores.append(jnp.dot(
                        jnp.concatenate([high, low], axis=1), key_stage[:, :rows],
                        preferred_element_type=jnp.float32,
                    ))
                for stream in range(STREAMS):
                    pair = places[stream * PAIR:(stream + 1) * PAIR]
                    far, close = scores[stream][:, :prefix_rows], scores[stream][:, prefix_rows:] + shade
                    lanes = [far[:, k:k + HD] for k in range(0, prefix_rows, HD)]
                    lanes += [close[:, k:k + HD] for k in range(0, near_rows, HD)]
                    top = jnp.max(functools.reduce(jnp.maximum, lanes), axis=1, keepdims=True)
                    weights = jnp.concatenate([
                        jnp.exp2(far - top).astype(jnp.bfloat16),
                        jnp.exp2(close - top).astype(jnp.bfloat16),
                    ], axis=1)
                    total = jnp.dot(
                        weights, value_stage[:rows, :], preferred_element_type=jnp.float32
                    )
                    for k, place in enumerate(pair):
                        part = total[k * half_rows:(k + 1) * half_rows]
                        result = jnp.where(live, part[:, :HD] / part[:, HD:], 0.0)
                        out[span, place] = result.astype(out.dtype)
                if h + 1 < heads:
                    done = (half * chunks + i + 1) * layers
                    for k in range(1, max(1, layers // slots) + 1):
                        @pl.when(done % slots == 0)
                        def _(k=k):
                            relay(h + 1, done // slots - max(1, layers // slots) + k)

    @pl.when(me + 1 < reqs)
    def _():
        before_copy.wait_send()

    for h in range(heads):
        for k in range(1, tps):
            peer_copy(h, (tp + k) % tps, tp).wait_send()

        @pl.loop(0, layers)
        def _(layer, h=h):
            mine = layer * 4 + x * 2 + core

            @pl.when((layer <= z) & (z + 1 < layers))
            def _():
                unit_copy(h, mine, UP).wait_send()

            @pl.when((layer >= z) & (z > 0))
            def _():
                unit_copy(h, mine, DOWN).wait_send()

            unit_copy(h, mine, ACROSS).wait_send()
            unit_copy(h, mine, SIBLING).wait_send()
            unit_copy(h, layer * 4 + (1 - x) * 2 + core, SIBLING).wait_send()


def per_device(reqs, tps, queries, suffix, prefix, lengths, groups, order, owners):
    heads = suffix.shape[2] // HD
    rows = queries.shape[0]
    half = rows // 2
    block_rows = prefix.shape[2] * tps
    keys = reqs // GROUPS * block_rows + rows
    vmem = pl.BlockSpec(memory_space=pltpu.VMEM)
    smem = pl.BlockSpec(memory_space=pltpu.SMEM)
    return pl.pallas_call(
        functools.partial(kernel, reqs, tps, heads),
        out_shape=jax.ShapeDtypeStruct(queries.shape, queries.dtype),
        in_specs=[vmem] * 3 + [smem] * 4,
        out_specs=vmem,
        scratch_shapes=[pltpu.VMEM((reqs, 2, block_rows, HD), jnp.bfloat16)] * heads + [
            pltpu.VMEM((2, half, suffix.shape[2]), jnp.bfloat16),
            pltpu.VMEM((2 * HD, keys), jnp.bfloat16),
            pltpu.VMEM((keys, 2 * HD), jnp.bfloat16),
            pltpu.VMEM((2, half, rows), jnp.float32),
            pltpu.SemaphoreType.DMA((heads, reqs, 4)),
            pltpu.SemaphoreType.DMA((heads, reqs)),
            pltpu.SemaphoreType.DMA((heads, tps)),
            pltpu.SemaphoreType.DMA((heads, tps)),
            pltpu.SemaphoreType.DMA((heads,)),
            pltpu.SemaphoreType.DMA,
            pltpu.SemaphoreType.DMA,
        ],
        compiler_params=pltpu.CompilerParams(
            collective_id=0, has_side_effects=True, vmem_limit_bytes=56 * 1024 * 1024
        ),
        cost_estimate=pl.CostEstimate(
            flops=4 * rows * heads * PER_KV * HD * keys,
            bytes_accessed=4 * queries.size,
            transcendentals=rows * heads * PER_KV * keys,
        ),
    )(queries, suffix, prefix, lengths, groups, order, owners)


def solution(mesh):
    in_specs = (
        P("req", "tp"),
        P(None, "req", "tp"),
        P(None, "req", "tp", None),
        P(),
        P(),
        P(),
        P(),
    )
    body = functools.partial(per_device, mesh.shape["req"], mesh.shape["tp"])
    return jax.shard_map(
        body, mesh=mesh, in_specs=in_specs, out_specs=P("req", "tp"), check_vma=False
    )
```

```python
import functools
import math

import jax
import jax.numpy as jnp
from jax import lax
from jax.experimental import pallas as pl
from jax.experimental.pallas import tpu as pltpu
from jax.sharding import PartitionSpec as P

QH = 64
KVH = 8
HD = 128
GROUPS = 4
PER_KV = QH // KVH
PAIR = 4
TILE = 256
BLOCK = 16
UP, DOWN, ACROSS, SIBLING = range(4)

masked_score = -1e30
to_exp2 = math.log2(math.e) / math.sqrt(HD)


def nt_dot(a, b):
    return lax.dot_general(a, b, (((1,), (1,)), ((), ())), preferred_element_type=jnp.float32)


def kernel(
    reqs, tps, heads,
    queries, suffix, prefix, lengths, groups, order, owners,
    out,
    *scratch,
):
    stored = scratch[:heads]
    (before, key_stage, value_stage, bias, scores, weights,
     unit_send, unit_recv, peer_send, peer_recv, own_sem, before_send, before_recv) = scratch[heads:]
    me = lax.axis_index("req")
    tp = lax.axis_index("tp")
    layers = reqs // 4
    z, x, core = me // 4, (me // 2) % 2, me % 2
    half_rows = queries.shape[0] // 2
    block_rows = stored[0].shape[2]
    part_rows = block_rows // tps
    per_group = reqs // GROUPS
    prefix_rows = per_group * block_rows
    across = z * 4 + (1 - x) * 2 + core
    sibling = z * 4 + x * 2 + 1 - core
    targets = {UP: me + 4, DOWN: me - 4, ACROSS: across, SIBLING: sibling}

    barrier = pltpu.get_barrier_semaphore()

    def greet(there, **device):
        @pl.when(there)
        def _():
            pl.semaphore_signal(barrier, inc=1, device_id=device, device_id_type=pl.DeviceIdType.MESH)

        return jnp.where(there, 1, 0)

    met = (
        greet(z + 1 < layers, req=me + 4)
        + greet(z > 0, req=me - 4)
        + greet(z >= 0, req=across)
        + greet(z >= 0, req=sibling)
        + greet((core == 1) & (me + 1 < reqs), req=me + 1)
        + greet((core == 0) & (me > 0), req=me - 1)
    )
    for k in range(1, tps):
        met = met + greet(z >= 0, tp=(tp + k) % tps)
    pl.semaphore_wait(barrier, met)

    def unit_copy(h, block, way):
        return pltpu.make_async_remote_copy(
            src_ref=stored[h].at[block],
            dst_ref=stored[h].at[block],
            send_sem=unit_send.at[h, block, way],
            recv_sem=unit_recv.at[h, block],
            device_id={"req": targets[way]},
            device_id_type=pl.DeviceIdType.MESH,
        )

    def peer_copy(h, peer, part):
        columns = pl.ds(pl.multiple_of((peer * heads + h) * HD, HD), HD)
        return pltpu.make_async_remote_copy(
            src_ref=prefix.at[:, 0, :, columns],
            dst_ref=stored[h].at[me, :, pl.ds(pl.multiple_of(part * part_rows, part_rows), part_rows), :],
            send_sem=peer_send.at[h, peer],
            recv_sem=peer_recv.at[h, part],
            device_id={"tp": peer},
            device_id_type=pl.DeviceIdType.MESH,
        )

    def own_copy(h):
        columns = pl.ds(pl.multiple_of((tp * heads + h) * HD, HD), HD)
        return pltpu.make_async_copy(
            prefix.at[:, 0, :, columns],
            stored[h].at[me, :, pl.ds(pl.multiple_of(tp * part_rows, part_rows), part_rows), :],
            own_sem.at[h],
        )

    before_copy = pltpu.make_async_remote_copy(
        src_ref=suffix.at[:, pl.ds(half_rows, half_rows), :],
        dst_ref=before,
        send_sem=before_send,
        recv_sem=before_recv,
        device_id={"req": me + 1},
        device_id_type=pl.DeviceIdType.MESH,
    )

    def pass_on(h, block, ways):
        for way, there in ways:
            @pl.when(there)
            def _(way=way):
                unit_copy(h, block, way).start()

    def send_own(h):
        own_copy(h).wait()
        for k in range(1, tps):
            peer_copy(h, (tp + k) % tps, (tp + k) % tps).wait_recv()
        pass_on(h, me, [(UP, z + 1 < layers), (DOWN, z > 0), (ACROSS, z >= 0), (SIBLING, z >= 0)])

    def from_layer(h, step):
        below, above = z - step, z + step

        @pl.when(below >= 0)
        def _():
            block = me - 4 * step
            unit_copy(h, block, UP).wait_recv()
            pass_on(h, block, [(UP, z + 1 < layers), (ACROSS, z >= 0), (SIBLING, z >= 0)])

        @pl.when(above < layers)
        def _():
            block = me + 4 * step
            unit_copy(h, block, DOWN).wait_recv()
            pass_on(h, block, [(DOWN, z > 0), (ACROSS, z >= 0), (SIBLING, z >= 0)])

    def from_across(h, step):
        below, above = z - step, z + step

        @pl.when(below >= 0)
        def _():
            unit_copy(h, across - 4 * step, ACROSS).wait_recv()
            unit_copy(h, across - 4 * step, SIBLING).start()

        @pl.when((above < layers) & (step > 0))
        def _():
            unit_copy(h, across + 4 * step, ACROSS).wait_recv()
            unit_copy(h, across + 4 * step, SIBLING).start()

    def relay(h, step):
        @pl.when(step < layers)
        def _():
            from_layer(h, step)

        from_across(h, step - 1)

    def from_sibling(h):
        @pl.loop(0, reqs // 2)
        def _(i):
            unit_copy(h, i * 2 + 1 - core, SIBLING).wait_recv()

    for h in range(heads):
        own_copy(h).start()
        for k in range(1, tps):
            peer_copy(h, (tp + k) % tps, tp).start()
    send_own(0)

    @pl.when(me + 1 < reqs)
    def _():
        before_copy.start()

    if heads > 1:
        send_own(1)

    tail = order[jnp.maximum(me - 1, 0)]
    head = order[jnp.minimum(me, reqs - 2)]
    tail_length = jnp.where(me > 0, lengths[tail], 0)
    head_length = jnp.where(me + 1 < reqs, lengths[head], 0)
    group_of = (groups[tail], groups[head])
    tail_live = tail_length - tail_length // 2
    tail_first = half_rows - tail_length // 2
    head_first = half_rows - head_length // 2
    near = bias.shape[2]
    head_near = 4 * half_rows // 3
    row = lax.broadcasted_iota(jnp.int32, (half_rows, near), 0)
    column = lax.broadcasted_iota(jnp.int32, (half_rows, near), 1)
    seen = (column >= tail_first) & (column - half_rows <= row)
    bias[0] = jnp.where(seen, 0.0, masked_score)
    own_column = column - (head_near - half_rows)
    seen = (own_column >= head_first) & (own_column <= row)
    bias[1] = jnp.where(seen, 0.0, masked_score)
    slot = lax.broadcasted_iota(jnp.int32, (half_rows, HD), 0)
    value_stage[:, HD:] = jnp.ones((value_stage.shape[0], HD), value_stage.dtype)

    @pl.when(me == 0)
    def _():
        before[...] = jnp.zeros(before.shape, before.dtype)

    for step in range(1, layers + 1):
        relay(0, step)

    @pl.when(me > 0)
    def _():
        before_copy.wait_recv()

    chunks = PER_KV // PAIR
    slots = 2 * chunks
    for h in range(heads):
        from_sibling(h)
        own_columns = slice(h * HD, (h + 1) * HD)
        if h + 2 < heads:
            send_own(h + 2)
        for half in range(2):
            for i in range(per_group):
                block = owners[group_of[half] * per_group + i]
                rows = slice(i * block_rows, (i + 1) * block_rows)
                turned = stored[h][block, 0].T
                key_stage[:HD, rows] = turned
                key_stage[HD:, rows] = turned
                value_stage[rows, :HD] = stored[h][block, 1]
            near_rows = near if half == 0 else head_near
            if half == 0:
                close = [
                    jnp.concatenate(
                        [before[kind, :, own_columns], suffix[kind, :half_rows, own_columns]], axis=0
                    ) for kind in range(2)
                ]
            else:
                close = [suffix[kind, 2 * half_rows - near_rows:, own_columns] for kind in range(2)]
            rows = slice(prefix_rows, prefix_rows + near_rows)
            turned = close[0].T
            key_stage[:HD, rows] = turned
            key_stage[HD:, rows] = turned
            value_stage[rows, :HD] = close[1]
            live = slot < tail_live if half == 0 else slot >= head_first

            @pl.loop(0, chunks)
            def _(i, half=half, near_rows=near_rows, live=live, h=h):
                span = pl.ds(half * half_rows, half_rows)
                first = (h * PER_KV + i * PAIR) * HD
                places = [
                    pl.ds(pl.multiple_of(first + k * HD, HD), HD) for k in range(PAIR)
                ]
                shade = jnp.concatenate([bias[half][:, :near_rows]] * PAIR, axis=0)
                rows = prefix_rows + near_rows
                query = jnp.concatenate([queries[span, place] for place in places], axis=0)
                query = query.astype(jnp.float32) * to_exp2
                high = query.astype(jnp.bfloat16)
                low = (query - high.astype(jnp.float32)).astype(jnp.bfloat16)
                query = jnp.concatenate([high, low], axis=1)
                for first in range(0, rows, TILE):
                    tile = slice(first, min(first + TILE, rows))
                    part = jnp.dot(query, key_stage[:, tile], preferred_element_type=jnp.float32)
                    if first >= prefix_rows:
                        part = part + shade[:, first - prefix_rows:tile.stop - prefix_rows]
                    scores[:, tile] = part
                for first in range(0, scores.shape[0], BLOCK):
                    block = slice(first, first + BLOCK)
                    score = scores[block, :rows]
                    lanes = [score[:, k:k + HD] for k in range(0, rows, HD)]
                    top = jnp.max(functools.reduce(jnp.maximum, lanes), axis=1, keepdims=True)
                    weights[block, :rows] = jnp.exp2(score - top).astype(jnp.bfloat16)
                total = jnp.dot(
                    weights[:, :rows], value_stage[:rows, :], preferred_element_type=jnp.float32
                )
                for k, place in enumerate(places):
                    part = total[k * half_rows:(k + 1) * half_rows]
                    result = jnp.where(live, part[:, :HD] / part[:, HD:], 0.0)
                    out[span, place] = result.astype(out.dtype)
                if h + 1 < heads:
                    done = (half * chunks + i + 1) * layers
                    for k in range(1, max(1, layers // slots) + 1):
                        @pl.when(done % slots == 0)
                        def _(k=k):
                            relay(h + 1, done // slots - max(1, layers // slots) + k)

    @pl.when(me + 1 < reqs)
    def _():
        before_copy.wait_send()

    for h in range(heads):
        for k in range(1, tps):
            peer_copy(h, (tp + k) % tps, tp).wait_send()

        @pl.loop(0, layers)
        def _(layer, h=h):
            mine = layer * 4 + x * 2 + core

            @pl.when((layer <= z) & (z + 1 < layers))
            def _():
                unit_copy(h, mine, UP).wait_send()

            @pl.when((layer >= z) & (z > 0))
            def _():
                unit_copy(h, mine, DOWN).wait_send()

            unit_copy(h, mine, ACROSS).wait_send()
            unit_copy(h, mine, SIBLING).wait_send()
            unit_copy(h, layer * 4 + (1 - x) * 2 + core, SIBLING).wait_send()


def per_device(reqs, tps, queries, suffix, prefix, lengths, groups, order, owners):
    heads = suffix.shape[2] // HD
    rows = queries.shape[0]
    half = rows // 2
    block_rows = prefix.shape[2] * tps
    keys = reqs // GROUPS * block_rows + rows
    vmem = pl.BlockSpec(memory_space=pltpu.VMEM)
    smem = pl.BlockSpec(memory_space=pltpu.SMEM)
    return pl.pallas_call(
        functools.partial(kernel, reqs, tps, heads),
        out_shape=jax.ShapeDtypeStruct(queries.shape, queries.dtype),
        in_specs=[vmem] * 3 + [smem] * 4,
        out_specs=vmem,
        scratch_shapes=[pltpu.VMEM((reqs, 2, block_rows, HD), jnp.bfloat16)] * heads + [
            pltpu.VMEM((2, half, suffix.shape[2]), jnp.bfloat16),
            pltpu.VMEM((2 * HD, keys), jnp.bfloat16),
            pltpu.VMEM((keys, 2 * HD), jnp.bfloat16),
            pltpu.VMEM((2, half, rows), jnp.float32),
            pltpu.VMEM((PAIR * half, keys), jnp.float32),
            pltpu.VMEM((PAIR * half, keys), jnp.bfloat16),
            pltpu.SemaphoreType.DMA((heads, reqs, 4)),
            pltpu.SemaphoreType.DMA((heads, reqs)),
            pltpu.SemaphoreType.DMA((heads, tps)),
            pltpu.SemaphoreType.DMA((heads, tps)),
            pltpu.SemaphoreType.DMA((heads,)),
            pltpu.SemaphoreType.DMA,
            pltpu.SemaphoreType.DMA,
        ],
        compiler_params=pltpu.CompilerParams(
            collective_id=0, has_side_effects=True, vmem_limit_bytes=56 * 1024 * 1024
        ),
        cost_estimate=pl.CostEstimate(
            flops=4 * rows * heads * PER_KV * HD * keys,
            bytes_accessed=4 * queries.size,
            transcendentals=rows * heads * PER_KV * keys,
        ),
    )(queries, suffix, prefix, lengths, groups, order, owners)


def solution(mesh):
    in_specs = (
        P("req", "tp"),
        P(None, "req", "tp"),
        P(None, "req", "tp", None),
        P(),
        P(),
        P(),
        P(),
    )
    body = functools.partial(per_device, mesh.shape["req"], mesh.shape["tp"])
    return jax.shard_map(
        body, mesh=mesh, in_specs=in_specs, out_specs=P("req", "tp"), check_vma=False
    )
```

```python
import functools
import math

import jax
import jax.numpy as jnp
from jax import lax
from jax.experimental import pallas as pl
from jax.experimental.pallas import tpu as pltpu
from jax.sharding import PartitionSpec as P

QH = 64
KVH = 8
HD = 128
GROUPS = 4
PER_KV = QH // KVH
PAIR = 2
STREAMS = 2
UP, DOWN, ACROSS, SIBLING = range(4)

masked_score = -1e30
to_exp2 = math.log2(math.e) / math.sqrt(HD)


def nt_dot(a, b):
    return lax.dot_general(a, b, (((1,), (1,)), ((), ())), preferred_element_type=jnp.float32)


def kernel(
    reqs, tps, heads,
    queries, suffix, prefix, lengths, groups, order, owners,
    out,
    *scratch,
):
    stored = scratch[:heads]
    (before, key_stage, value_stage, bias,
     unit_send, unit_recv, peer_send, peer_recv, own_sem, before_send, before_recv) = scratch[heads:]
    me = lax.axis_index("req")
    tp = lax.axis_index("tp")
    layers = reqs // 4
    z, x, core = me // 4, (me // 2) % 2, me % 2
    half_rows = queries.shape[0] // 2
    block_rows = stored[0].shape[2]
    part_rows = block_rows // tps
    per_group = reqs // GROUPS
    prefix_rows = per_group * block_rows
    across = z * 4 + (1 - x) * 2 + core
    sibling = z * 4 + x * 2 + 1 - core
    targets = {UP: me + 4, DOWN: me - 4, ACROSS: across, SIBLING: sibling}

    barrier = pltpu.get_barrier_semaphore()

    def greet(there, **device):
        @pl.when(there)
        def _():
            pl.semaphore_signal(barrier, inc=1, device_id=device, device_id_type=pl.DeviceIdType.MESH)

        return jnp.where(there, 1, 0)

    met = (
        greet(z + 1 < layers, req=me + 4)
        + greet(z > 0, req=me - 4)
        + greet(z >= 0, req=across)
        + greet(z >= 0, req=sibling)
        + greet((core == 1) & (me + 1 < reqs), req=me + 1)
        + greet((core == 0) & (me > 0), req=me - 1)
    )
    for k in range(1, tps):
        met = met + greet(z >= 0, tp=(tp + k) % tps)
    pl.semaphore_wait(barrier, met)

    def unit_copy(h, block, way):
        return pltpu.make_async_remote_copy(
            src_ref=stored[h].at[block],
            dst_ref=stored[h].at[block],
            send_sem=unit_send.at[h, block, way],
            recv_sem=unit_recv.at[h, block],
            device_id={"req": targets[way]},
            device_id_type=pl.DeviceIdType.MESH,
        )

    def peer_copy(h, peer, part):
        columns = pl.ds(pl.multiple_of((peer * heads + h) * HD, HD), HD)
        return pltpu.make_async_remote_copy(
            src_ref=prefix.at[:, 0, :, columns],
            dst_ref=stored[h].at[me, :, pl.ds(pl.multiple_of(part * part_rows, part_rows), part_rows), :],
            send_sem=peer_send.at[h, peer],
            recv_sem=peer_recv.at[h, part],
            device_id={"tp": peer},
            device_id_type=pl.DeviceIdType.MESH,
        )

    def own_copy(h):
        columns = pl.ds(pl.multiple_of((tp * heads + h) * HD, HD), HD)
        return pltpu.make_async_copy(
            prefix.at[:, 0, :, columns],
            stored[h].at[me, :, pl.ds(pl.multiple_of(tp * part_rows, part_rows), part_rows), :],
            own_sem.at[h],
        )

    before_copy = pltpu.make_async_remote_copy(
        src_ref=suffix.at[:, pl.ds(half_rows, half_rows), :],
        dst_ref=before,
        send_sem=before_send,
        recv_sem=before_recv,
        device_id={"req": me + 1},
        device_id_type=pl.DeviceIdType.MESH,
    )

    def pass_on(h, block, ways):
        for way, there in ways:
            @pl.when(there)
            def _(way=way):
                unit_copy(h, block, way).start()

    def send_own(h):
        own_copy(h).wait()
        for k in range(1, tps):
            peer_copy(h, (tp + k) % tps, (tp + k) % tps).wait_recv()
        pass_on(h, me, [(UP, z + 1 < layers), (DOWN, z > 0), (ACROSS, z >= 0), (SIBLING, z >= 0)])

    def from_layer(h, step):
        below, above = z - step, z + step

        @pl.when(below >= 0)
        def _():
            block = me - 4 * step
            unit_copy(h, block, UP).wait_recv()
            pass_on(h, block, [(UP, z + 1 < layers), (ACROSS, z >= 0), (SIBLING, z >= 0)])

        @pl.when(above < layers)
        def _():
            block = me + 4 * step
            unit_copy(h, block, DOWN).wait_recv()
            pass_on(h, block, [(DOWN, z > 0), (ACROSS, z >= 0), (SIBLING, z >= 0)])

    def from_across(h, step):
        below, above = z - step, z + step

        @pl.when(below >= 0)
        def _():
            unit_copy(h, across - 4 * step, ACROSS).wait_recv()
            unit_copy(h, across - 4 * step, SIBLING).start()

        @pl.when((above < layers) & (step > 0))
        def _():
            unit_copy(h, across + 4 * step, ACROSS).wait_recv()
            unit_copy(h, across + 4 * step, SIBLING).start()

    def relay(h, step):
        @pl.when(step < layers)
        def _():
            from_layer(h, step)

        from_across(h, step - 1)

    def from_sibling(h):
        @pl.loop(0, reqs // 2)
        def _(i):
            unit_copy(h, i * 2 + 1 - core, SIBLING).wait_recv()

    for h in range(heads):
        own_copy(h).start()
        for k in range(1, tps):
            peer_copy(h, (tp + k) % tps, tp).start()
    send_own(0)

    @pl.when(me + 1 < reqs)
    def _():
        before_copy.start()

    if heads > 1:
        send_own(1)

    tail = order[jnp.maximum(me - 1, 0)]
    head = order[jnp.minimum(me, reqs - 2)]
    tail_length = jnp.where(me > 0, lengths[tail], 0)
    head_length = jnp.where(me + 1 < reqs, lengths[head], 0)
    group_of = (groups[tail], groups[head])
    tail_live = tail_length - tail_length // 2
    tail_first = half_rows - tail_length // 2
    head_first = half_rows - head_length // 2
    near = bias.shape[2]
    row = lax.broadcasted_iota(jnp.int32, (half_rows, near), 0)
    column = lax.broadcasted_iota(jnp.int32, (half_rows, near), 1)
    seen = (column >= tail_first) & (column - half_rows <= row)
    bias[0] = jnp.where(seen, 0.0, masked_score)
    own_column = column - (near - half_rows)
    seen = (own_column >= head_first) & (own_column <= row)
    bias[1] = jnp.where(seen, 0.0, masked_score)
    slot = lax.broadcasted_iota(jnp.int32, (half_rows, HD), 0)
    value_stage[:, HD:] = jnp.ones((value_stage.shape[0], HD), value_stage.dtype)

    @pl.when(me == 0)
    def _():
        before[...] = jnp.zeros(before.shape, before.dtype)

    for step in range(1, layers + 1):
        relay(0, step)

    @pl.when(me > 0)
    def _():
        before_copy.wait_recv()

    chunks = PER_KV // (PAIR * STREAMS)
    slots = 2 * chunks
    @pl.loop(0, 2 * heads)
    def _(turn):
        h, half = turn // 2, turn % 2
        group = jnp.where(half == 0, group_of[0], group_of[1])
        for k in range(heads):
            @pl.when(turn == 2 * k)
            def _(k=k):
                from_sibling(k)
                if k + 2 < heads:
                    send_own(k + 2)

            @pl.when(h == k)
            def _(k=k):
                for i in range(per_group):
                    block = owners[group * per_group + i]
                    rows = slice(i * block_rows, (i + 1) * block_rows)
                    turned = stored[k][block, 0].T
                    key_stage[:HD, rows] = turned
                    key_stage[HD:, rows] = turned
                    value_stage[rows, :HD] = stored[k][block, 1]

        own_columns = pl.ds(pl.multiple_of(h * HD, HD), HD)
        rows = slice(prefix_rows, prefix_rows + near)

        def stage_near(keys, values):
            turned = keys.T
            key_stage[:HD, rows] = turned
            key_stage[HD:, rows] = turned
            value_stage[rows, :HD] = values

        @pl.when(half == 0)
        def _():
            stage_near(*[
                jnp.concatenate(
                    [before[kind, :, own_columns], suffix[kind, :half_rows, own_columns]], axis=0
                ) for kind in range(2)
            ])

        @pl.when(half == 1)
        def _():
            stage_near(suffix[0, :, own_columns], suffix[1, :, own_columns])

        live = (slot >= jnp.where(half == 0, 0, head_first)) & (
            slot < jnp.where(half == 0, tail_live, half_rows)
        )

        @pl.loop(0, chunks)
        def _(i):
            span = pl.ds(pl.multiple_of(half * half_rows, half_rows), half_rows)
            first = (h * PER_KV + i * PAIR * STREAMS) * HD
            places = [
                pl.ds(pl.multiple_of(first + k * HD, HD), HD) for k in range(PAIR * STREAMS)
            ]
            shade = jnp.concatenate([bias[half]] * PAIR, axis=0)
            rows = prefix_rows + near
            scores = []
            for stream in range(STREAMS):
                pair = places[stream * PAIR:(stream + 1) * PAIR]
                query = jnp.concatenate([queries[span, place] for place in pair], axis=0)
                query = query.astype(jnp.float32) * to_exp2
                high = query.astype(jnp.bfloat16)
                low = (query - high.astype(jnp.float32)).astype(jnp.bfloat16)
                scores.append(jnp.dot(
                    jnp.concatenate([high, low], axis=1), key_stage[:, :rows],
                    preferred_element_type=jnp.float32,
                ))
            for stream in range(STREAMS):
                pair = places[stream * PAIR:(stream + 1) * PAIR]
                far, close = scores[stream][:, :prefix_rows], scores[stream][:, prefix_rows:] + shade
                lanes = [far[:, k:k + HD] for k in range(0, prefix_rows, HD)]
                lanes += [close[:, k:k + HD] for k in range(0, near, HD)]
                top = jnp.max(functools.reduce(jnp.maximum, lanes), axis=1, keepdims=True)
                weights = jnp.concatenate([
                    jnp.exp2(far - top).astype(jnp.bfloat16),
                    jnp.exp2(close - top).astype(jnp.bfloat16),
                ], axis=1)
                total = jnp.dot(
                    weights, value_stage[:rows, :], preferred_element_type=jnp.float32
                )
                for k, place in enumerate(pair):
                    part = total[k * half_rows:(k + 1) * half_rows]
                    result = jnp.where(live, part[:, :HD] / part[:, HD:], 0.0)
                    out[span, place] = result.astype(out.dtype)
            done = (half * chunks + i + 1) * layers
            steps = max(1, layers // slots)
            for later in range(1, heads):
                @pl.when((h + 1 == later) & (done % slots == 0))
                def _(later=later):
                    for k in range(1, steps + 1):
                        relay(later, done // slots - steps + k)

    @pl.when(me + 1 < reqs)
    def _():
        before_copy.wait_send()

    for h in range(heads):
        for k in range(1, tps):
            peer_copy(h, (tp + k) % tps, tp).wait_send()

        @pl.loop(0, layers)
        def _(layer, h=h):
            mine = layer * 4 + x * 2 + core

            @pl.when((layer <= z) & (z + 1 < layers))
            def _():
                unit_copy(h, mine, UP).wait_send()

            @pl.when((layer >= z) & (z > 0))
            def _():
                unit_copy(h, mine, DOWN).wait_send()

            unit_copy(h, mine, ACROSS).wait_send()
            unit_copy(h, mine, SIBLING).wait_send()
            unit_copy(h, layer * 4 + (1 - x) * 2 + core, SIBLING).wait_send()


def per_device(reqs, tps, queries, suffix, prefix, lengths, groups, order, owners):
    heads = suffix.shape[2] // HD
    rows = queries.shape[0]
    half = rows // 2
    block_rows = prefix.shape[2] * tps
    keys = reqs // GROUPS * block_rows + rows
    vmem = pl.BlockSpec(memory_space=pltpu.VMEM)
    smem = pl.BlockSpec(memory_space=pltpu.SMEM)
    return pl.pallas_call(
        functools.partial(kernel, reqs, tps, heads),
        out_shape=jax.ShapeDtypeStruct(queries.shape, queries.dtype),
        in_specs=[vmem] * 3 + [smem] * 4,
        out_specs=vmem,
        scratch_shapes=[pltpu.VMEM((reqs, 2, block_rows, HD), jnp.bfloat16)] * heads + [
            pltpu.VMEM((2, half, suffix.shape[2]), jnp.bfloat16),
            pltpu.VMEM((2 * HD, keys), jnp.bfloat16),
            pltpu.VMEM((keys, 2 * HD), jnp.bfloat16),
            pltpu.VMEM((2, half, rows), jnp.float32),
            pltpu.SemaphoreType.DMA((heads, reqs, 4)),
            pltpu.SemaphoreType.DMA((heads, reqs)),
            pltpu.SemaphoreType.DMA((heads, tps)),
            pltpu.SemaphoreType.DMA((heads, tps)),
            pltpu.SemaphoreType.DMA((heads,)),
            pltpu.SemaphoreType.DMA,
            pltpu.SemaphoreType.DMA,
        ],
        compiler_params=pltpu.CompilerParams(
            collective_id=0, has_side_effects=True, vmem_limit_bytes=56 * 1024 * 1024
        ),
        cost_estimate=pl.CostEstimate(
            flops=4 * rows * heads * PER_KV * HD * keys,
            bytes_accessed=4 * queries.size,
            transcendentals=rows * heads * PER_KV * keys,
        ),
    )(queries, suffix, prefix, lengths, groups, order, owners)


def solution(mesh):
    in_specs = (
        P("req", "tp"),
        P(None, "req", "tp"),
        P(None, "req", "tp", None),
        P(),
        P(),
        P(),
        P(),
    )
    body = functools.partial(per_device, mesh.shape["req"], mesh.shape["tp"])
    return jax.shard_map(
        body, mesh=mesh, in_specs=in_specs, out_specs=P("req", "tp"), check_vma=False
    )
```
